512 devices in a mesh: context: 64 (over y_hi, z, core), tensor: 8 (over x, y_lo).
Axes of the slice: x: 4, y: 8 (y_hi: 4, y_lo: 2; y = y_hi * 2 + y_lo), z: 8, core: 2. Of those that a mesh axis runs over, the one named last changes fastest.
Arguments:
- in_gate: bfloat16 [16384, 2048], P('context', 'tensor'), may hold values from -6 to 6
- out_gate: bfloat16 [16384, 2048], P('context', 'tensor'), may hold values from -6 to 6
- values: bfloat16 [16384, 2048], P('context', 'tensor'), may hold values from -6 to 6
- long_filters: float32 [16384, 128], P('context', 'tensor'), may hold values from -1 to 1
- skip_gain: float32 [2048], P('tensor'), may hold values from 0.5 to 2
- projection: bfloat16 [2048, 2048], P('tensor'), may hold values from -0.1875 to 0.1875
Outputs:
- mixed_out: bfloat16 [16384, 2048], P('context', 'tensor')
The draws below stay inside these ranges and needn't reach their ends.
All inputs are finite; a program needn't handle non-finite values.
Results may differ from the reference program's by a relative error of at most 0.017.
Values may be sent and summed in bfloat16 or wider, within the bound.
No kernel may reach another device: no remote copies, remote signals or barrier semaphores. Data moves between devices by JAX's collectives and lax.ppermute only.
A program may use at most 64 MiB of HBM per device.

```python
import jax
import jax.numpy as jnp
from jax import lax

D = 2048
GROUPS = 128
SEQ = 16384
CH = 256
N_TENSOR = 8


def draw_long_filters(key, part):
    key = jax.random.fold_in(key, 11)
    first = jax.random.fold_in(key, 0)
    lags = jnp.arange(SEQ).astype(jnp.float32) / SEQ
    envelope = 1.5 - lags
    noise = jnp.clip(jax.random.normal(first, (SEQ, GROUPS), jnp.float32), -6.0, 6.0)
    return noise * envelope[:, None] * SEQ ** (-0.5)


def raised(values, rng, source, target, parts, factor):
    def block_of(position):
        return (jnp.arange(values.shape[position]) // (values.shape[position] // parts)).reshape((-1,) + (1,) * (values.ndim - 1 - position))

    first = jax.random.permutation(rng, parts)[block_of(target)]
    far = (block_of(target) + parts // 2) % parts
    return jnp.where((block_of(source) == first) | (block_of(source) == far), factor * values, values)


def levels(own_key, extent, cuts, low, high):
    def one(axis_at, parts):
        heights = jax.random.uniform(jax.random.fold_in(jax.random.fold_in(own_key, 6), axis_at), (parts,), jnp.float32, low / len(cuts), high / len(cuts))
        return jnp.repeat(jnp.exp(heights), extent[axis_at] // parts).reshape((-1,) + (1,) * (len(extent) - axis_at - 1))

    loudness = one(*cuts[0])
    for cut in cuts[1:]:
        loudness = loudness * one(*cut)
    return loudness


def scatter_about(stream_key, dims, width, limit, cuts=(), held_as=jnp.bfloat16):
    values = jax.random.normal(stream_key, dims, jnp.float32) * width
    if len(cuts) > 0:
        values = levels(stream_key, dims, cuts, -0.22, 0.18) * values
    return jnp.clip(values, min=-limit, max=limit).astype(held_as)


def bell_draw_with(key, dims, deviation, limit, cuts, heavy, dtype=jnp.bfloat16):
    entries = deviation * jax.random.normal(key, dims, jnp.float32)
    if cuts:
        entries = entries * levels(key, dims, cuts, -0.22, 0.18)
    return jnp.clip(raised(entries, jax.random.fold_in(key, 3), *heavy), -limit, limit).astype(dtype)


def setup_inputs(seed: int = 0) -> dict:
    key_of = jax.random.split(jax.random.key(seed), 7)
    return {
        "in_gate": scatter_about(key_of[0], (SEQ, D), 1.0, 6.0, ((0, 64), (1, 8))),
        "out_gate": scatter_about(key_of[1], (SEQ, D), 1.0, 6.0, ((0, 64), (1, 8))),
        "values": scatter_about(key_of[2], (SEQ, D), 1.0, 6.0, ((0, 64), (1, 8))),
        "long_filters": draw_long_filters(jax.random.fold_in(key_of[6], 71), 0),
        "skip_gain": jnp.clip(0.5 + 1.5 * jax.random.uniform(key_of[4], (D,), jnp.float32) ** levels(key_of[4], (D,), ((0, 8),), -0.2, 0.2), 0.5, 2.0),
        "projection": bell_draw_with(key_of[5], (D, D), D ** -0.5, 0.1875, ((0, 8),), (0, 1, 8, 2.0)),
    }


def reference(in_gate, out_gate, values, long_filters, skip_gain, projection):
    mixed = in_gate.astype(jnp.float32) * values.astype(jnp.float32)
    kernel_spec = jnp.fft.rfft(long_filters, n=2 * SEQ, axis=0)
    grouped = mixed.reshape(SEQ, GROUPS, D // GROUPS).transpose(1, 0, 2)

    def one_group(item):
        cols, spec = item
        signal_spec = jnp.fft.rfft(cols, n=2 * SEQ, axis=0)
        return jnp.fft.irfft(signal_spec * spec[:, None], n=2 * SEQ, axis=0)[:SEQ]

    conv = lax.map(one_group, (grouped, kernel_spec.T)).transpose(1, 0, 2).reshape(SEQ, D)
    combined = conv + skip_gain[None, :] * mixed
    gated = (combined * out_gate.astype(jnp.float32)).astype(jnp.bfloat16)
    pieces = gated.reshape(SEQ, N_TENSOR, CH).transpose(1, 0, 2)
    weights = projection.reshape(N_TENSOR, CH, D)

    def add_block(total, item):
        term = jnp.dot(item[0], item[1], preferred_element_type=jnp.float32).astype(jnp.bfloat16)
        term = lax.optimization_barrier(term)
        return total + term.astype(jnp.float32), None

    total, unused = lax.scan(add_block, jnp.zeros((SEQ, D), jnp.float32), (pieces, weights))
    return total.astype(jnp.bfloat16)
```

```python
import jax
import jax.numpy as jnp
from jax import lax
from jax.experimental import pallas as pl
from jax.experimental.pallas import tpu as pltpu
from jax.sharding import PartitionSpec as P

BLOCK = 128
SLOTS = 16
F32 = jnp.float32
BF16 = jnp.bfloat16


def iota(shape, axis):
    return lax.broadcasted_iota(jnp.int32, shape, axis)


def nt_dot(a, b):
    return lax.dot_general(a, b, (((1,), (1,)), ((), ())), preferred_element_type=F32)


def pack_kernel(in_gate_ref, values_ref, filters_ref, out_ref):
    rows, width = in_gate_ref.shape
    groups = filters_ref.shape[1]
    peers = out_ref.shape[0] // SLOTS
    chans = width // peers
    mixed = (in_gate_ref[...].astype(F32) * values_ref[...].astype(F32)).astype(BF16)
    filters = filters_ref[...].astype(BF16)
    total = None
    for b in range(rows // BLOCK):
        row, col = iota((peers * SLOTS, width), 0), iota((peers * SLOTS, width), 1)
        slot = row % SLOTS
        pick = (slot // chans == b) & ((row // SLOTS) * chans + slot % chans == col)
        part = nt_dot(pick.astype(F32).astype(BF16), mixed[b * BLOCK : (b + 1) * BLOCK])
        row, col = iota((peers * SLOTS, groups), 0), iota((peers * SLOTS, groups), 1)
        pick = (row % SLOTS == 8 + b) & (row // (SLOTS * peers // groups) == col)
        part += nt_dot(pick.astype(F32).astype(BF16), filters[b * BLOCK : (b + 1) * BLOCK])
        total = part if total is None else total + part
    out_ref[...] = total.astype(BF16)


def conv_kernel(in_ref, out_ref, lhs_ref, acc_ref, tap_ref):
    peers = in_ref.shape[0] // SLOTS
    blocks = 2 * peers
    rows = 4 * blocks
    half = blocks // 2
    received = in_ref[...].astype(F32).reshape(peers, 2, 8, BLOCK)
    x = received[:, 0].reshape(rows, BLOCK)
    tap_ref[...] = received[:, 1].reshape(peers * 8, BLOCK)
    for m in range(4):
        moved = x if m == 0 else jnp.concatenate([jnp.zeros((4 * m, BLOCK), F32), x[: rows - 4 * m]], axis=0)
        lhs_ref[:, m * BLOCK : (m + 1) * BLOCK] = moved.astype(BF16)
    acc_ref[...] = jnp.zeros_like(acc_ref)
    keep = iota((BLOCK, BLOCK), 1) >= iota((BLOCK, BLOCK), 0)

    def turned(block):
        if block < 0:
            return jnp.zeros((BLOCK, BLOCK), F32)
        place = (block // 2) * 8 + block % 2
        taps = jnp.broadcast_to(tap_ref[place : place + 1, :], (BLOCK, BLOCK))
        return pltpu.roll(taps, 0, 1, stride=1, stride_axis=0)

    last = {0: turned(-1), half: turned(half - 1)}
    for q in range(half // 4):
        sides = []
        for base in (0, half):
            stack = []
            for m in range(4):
                now = turned(base + 4 * q + m)
                stack.append(jnp.where(keep, now, last[base]).astype(BF16))
                last[base] = now
            sides.append(jnp.concatenate(stack, axis=0))
        near = 16 * q
        both = jnp.concatenate(sides, axis=1)
        mid = rows // 2
        acc_ref[near:mid, :] += jnp.dot(lhs_ref[: mid - near, :], both, preferred_element_type=F32)
        acc_ref[mid:, :BLOCK] += jnp.dot(lhs_ref[mid - near : rows - near, :], sides[0], preferred_element_type=F32)
    out_ref[: rows // 2, :] = acc_ref[: rows // 2, :BLOCK].astype(BF16)
    out_ref[rows // 2 :, :] = (acc_ref[rows // 2 :, :BLOCK] + acc_ref[: rows // 2, BLOCK:]).astype(BF16)


def project_kernel(conv_ref, in_gate_ref, values_ref, out_gate_ref, skip_ref, projection_ref, out_ref):
    rows, width = in_gate_ref.shape
    received = conv_ref[...].astype(F32).T.astype(BF16)
    parts = []
    for b in range(rows // BLOCK):
        row, col = iota((2 * width, width), 0), iota((2 * width, width), 1)
        pick = (row % 8 // 4 == b) & (row // 8 * 4 + row % 4 == col)
        parts.append(jnp.dot(received, pick.astype(F32).astype(BF16), preferred_element_type=F32))
    conv = jnp.concatenate(parts, axis=0)
    mixed = in_gate_ref[...].astype(F32) * values_ref[...].astype(F32)
    combined = conv + skip_ref[...] * mixed
    gated = (combined * out_gate_ref[...].astype(F32)).astype(BF16)
    for k in range(out_ref.shape[0]):
        out_ref[k] = jnp.dot(
            gated, projection_ref[:, k * width : (k + 1) * width], preferred_element_type=F32
        ).astype(BF16)


def sum_kernel(parts_ref, out_ref):
    total = parts_ref[0].astype(F32)
    for k in range(1, parts_ref.shape[0]):
        total += parts_ref[k].astype(F32)
    out_ref[...] = total.astype(BF16)


def call(kernel, shape, *args, scratch=()):
    return pl.pallas_call(
        kernel,
        out_shape=jax.ShapeDtypeStruct(shape, BF16),
        scratch_shapes=scratch,
        compiler_params=pltpu.CompilerParams(vmem_limit_bytes=32 * 1024 * 1024),
    )(*args)


def on_device(in_gate, out_gate, values, long_filters, skip_gain, projection):
    rows, width = in_gate.shape
    contexts = lax.axis_size("context")
    tensors = lax.axis_size("tensor")
    sent = call(pack_kernel, (contexts * SLOTS, BLOCK), in_gate, values, long_filters)
    held = lax.all_to_all(sent.reshape(contexts, SLOTS, BLOCK), "context", 0, 0, tiled=True)
    conv = call(
        conv_kernel,
        (contexts * 8, BLOCK),
        held.reshape(contexts * SLOTS, BLOCK),
        scratch=[
            pltpu.VMEM((contexts * 8, 4 * BLOCK), BF16),
            pltpu.VMEM((contexts * 8, 2 * BLOCK), F32),
            pltpu.VMEM((contexts * 8, BLOCK), F32),
        ],
    )
    back = lax.all_to_all(conv.reshape(contexts, 8, BLOCK), "context", 0, 0, tiled=True)
    partial = call(
        project_kernel,
        (tensors, rows, width),
        back.reshape(contexts * 8, BLOCK),
        in_gate,
        values,
        out_gate,
        skip_gain[None, :],
        projection,
    )
    shares = lax.all_to_all(partial, "tensor", 0, 0, tiled=True)
    return call(sum_kernel, (rows, width), shares)


def solution(mesh):
    return jax.shard_map(
        on_device,
        mesh=mesh,
        in_specs=(
            P("context", "tensor"),
            P("context", "tensor"),
            P("context", "tensor"),
            P("context", "tensor"),
            P("tensor"),
            P("tensor", None),
        ),
        out_specs=P("context", "tensor"),
        check_vma=False,
    )
```

```python
import jax
import jax.numpy as jnp
from jax import lax
from jax.experimental import pallas as pl
from jax.experimental.pallas import tpu as pltpu
from jax.sharding import PartitionSpec as P

BLOCK = 128
SLOTS = 10
F32 = jnp.float32
BF16 = jnp.bfloat16


def iota(shape, axis):
    return lax.broadcasted_iota(jnp.int32, shape, axis)


def nt_dot(a, b):
    return lax.dot_general(a, b, (((1,), (1,)), ((), ())), preferred_element_type=F32)


def pack_kernel(*refs):
    sources, (out_ref, direct_ref, out_gate_ref), refs = refs[:5], refs[5:8], refs[8:]
    in_gate_ref, values_ref, filters_ref, skip_ref, rows_ref, sems = refs
    targets = (in_gate_ref, values_ref, filters_ref, skip_ref, out_gate_ref)
    moves = [pltpu.make_async_copy(sources[n], targets[n], sems.at[n]) for n in range(5)]
    for move in moves:
        move.start()
    rows, width = in_gate_ref.shape
    groups = filters_ref.shape[0]
    peers = out_ref.shape[0] // SLOTS
    chans = width // peers
    row, col = iota((peers * 8, width), 0), iota((peers * 8, width), 1)
    picks = [
        ((row % 8 // chans == b) & (row // 8 * chans + row % chans == col)).astype(F32).astype(BF16) for b in range(2)
    ]
    for move in moves:
        move.wait()
    products = in_gate_ref[...].astype(F32) * values_ref[...].astype(F32)
    direct_ref[...] = skip_ref[...] * products
    mixed = products.astype(BF16)
    sent = sum(nt_dot(picks[b], mixed[b * BLOCK : (b + 1) * BLOCK]) for b in range(2))
    for j in range(peers):
        rows_ref[j * SLOTS : j * SLOTS + 8, :] = sent[j * 8 : j * 8 + 8]
        g = j // (peers // groups)
        for b in range(2):
            rows_ref[j * SLOTS + 8 + b : j * SLOTS + 9 + b, :] = filters_ref[g : g + 1, b * BLOCK : (b + 1) * BLOCK]
    out_ref[...] = rows_ref[...].astype(BF16)


def conv_kernel(in_ref, out_ref, lhs_ref, acc_ref, tap_ref):
    peers = in_ref.shape[0] // SLOTS
    blocks = 2 * peers
    rows = 4 * blocks
    half = blocks // 2
    tap_ref[...] = in_ref[...].astype(F32)
    x = jnp.concatenate([tap_ref[k * SLOTS : k * SLOTS + 8, :] for k in range(peers)], axis=0)
    for m in range(4):
        moved = x if m == 0 else jnp.concatenate([jnp.zeros((4 * m, BLOCK), F32), x[: rows - 4 * m]], axis=0)
        lhs_ref[:, m * BLOCK : (m + 1) * BLOCK] = moved.astype(BF16)
    acc_ref[...] = jnp.zeros_like(acc_ref)
    keep = iota((BLOCK, BLOCK), 1) >= iota((BLOCK, BLOCK), 0)

    def turned(block):
        if block < 0:
            return jnp.zeros((BLOCK, BLOCK), F32)
        place = (block // 2) * SLOTS + 8 + block % 2
        taps = jnp.broadcast_to(tap_ref[place : place + 1, :], (BLOCK, BLOCK))
        return pltpu.roll(taps, 0, 1, stride=1, stride_axis=0)

    last = {0: turned(-1), half: turned(half - 1)}
    for q in range(half // 4):
        sides = []
        for base in (0, half):
            stack = []
            for m in range(4):
                now = turned(base + 4 * q + m)
                stack.append(jnp.where(keep, now, last[base]).astype(BF16))
                last[base] = now
            sides.append(jnp.concatenate(stack, axis=0))
        near = 16 * q
        both = jnp.concatenate(sides, axis=1)
        mid = rows // 2
        acc_ref[near:mid, :] += jnp.dot(lhs_ref[: mid - near, :], both, preferred_element_type=F32)
        acc_ref[mid:, :BLOCK] += jnp.dot(lhs_ref[mid - near : rows - near, :], sides[0], preferred_element_type=F32)
    out_ref[: rows // 2, :] = acc_ref[: rows // 2, :BLOCK].astype(BF16)
    out_ref[rows // 2 :, :] = (acc_ref[rows // 2 :, :BLOCK] + acc_ref[: rows // 2, BLOCK:]).astype(BF16)


def project_kernel(conv_ref, direct_ref, out_gate_ref, projection_ref, out_ref):
    rows, width = direct_ref.shape
    received = conv_ref[...].astype(F32).T.astype(BF16)
    parts = []
    for b in range(rows // BLOCK):
        row, col = iota((2 * width, width), 0), iota((2 * width, width), 1)
        pick = (row % 8 // 4 == b) & (row // 8 * 4 + row % 4 == col)
        parts.append(jnp.dot(received, pick.astype(F32).astype(BF16), preferred_element_type=F32))
    conv = jnp.concatenate(parts, axis=0)
    gated = ((conv + direct_ref[...]) * out_gate_ref[...].astype(F32)).astype(BF16)
    for k in range(out_ref.shape[0]):
        out_ref[k] = jnp.dot(
            gated, projection_ref[:, k * width : (k + 1) * width], preferred_element_type=F32
        ).astype(BF16)


def sum_kernel(parts_ref, out_ref):
    total = parts_ref[0].astype(F32)
    for k in range(1, parts_ref.shape[0]):
        total += parts_ref[k].astype(F32)
    out_ref[...] = total.astype(BF16)


def call(kernel, shape, *args, scratch=()):
    return pl.pallas_call(
        kernel,
        out_shape=jax.ShapeDtypeStruct(shape, BF16),
        scratch_shapes=scratch,
        compiler_params=pltpu.CompilerParams(vmem_limit_bytes=32 * 1024 * 1024),
    )(*args)


def on_device(in_gate, out_gate, values, long_filters, skip_gain, projection):
    rows, width = in_gate.shape
    contexts = lax.axis_size("context")
    tensors = lax.axis_size("tensor")
    args = (in_gate, values, long_filters.T, skip_gain[None, :], out_gate)
    sent, direct, out_gate = pl.pallas_call(
        pack_kernel,
        in_specs=[pl.BlockSpec(memory_space=pltpu.HBM)] * len(args),
        out_shape=[
            jax.ShapeDtypeStruct((contexts * SLOTS, BLOCK), BF16),
            jax.ShapeDtypeStruct((rows, width), F32),
            jax.ShapeDtypeStruct((rows, width), BF16),
        ],
        scratch_shapes=[
            pltpu.VMEM((rows, width), BF16),
            pltpu.VMEM((rows, width), BF16),
            pltpu.VMEM((long_filters.shape[1], rows), F32),
            pltpu.VMEM((1, width), F32),
            pltpu.VMEM((contexts * SLOTS, BLOCK), F32),
            pltpu.SemaphoreType.DMA((len(args),)),
        ],
        compiler_params=pltpu.CompilerParams(vmem_limit_bytes=32 * 1024 * 1024),
    )(*(pltpu.with_memory_space_constraint(a, pltpu.HBM) for a in args))
    held = lax.all_to_all(sent.reshape(contexts * SLOTS // 2, 2, BLOCK), "context", 0, 0, tiled=True)
    conv = call(
        conv_kernel,
        (contexts * 8, BLOCK),
        held.reshape(contexts * SLOTS, BLOCK),
        scratch=[
            pltpu.VMEM((contexts * 8, 4 * BLOCK), BF16),
            pltpu.VMEM((contexts * 8, 2 * BLOCK), F32),
            pltpu.VMEM((contexts * SLOTS, BLOCK), F32),
        ],
    )
    back = lax.all_to_all(conv.reshape(contexts, 8, BLOCK), "context", 0, 0, tiled=True)
    partial = call(
        project_kernel,
        (tensors, rows, width),
        back.reshape(contexts * 8, BLOCK),
        direct,
        out_gate,
        projection,
    )
    shares = lax.all_to_all(partial, "tensor", 0, 0, tiled=True)
    return call(sum_kernel, (rows, width), shares)


def solution(mesh):
    return jax.shard_map(
        on_device,
        mesh=mesh,
        in_specs=(
            P("context", "tensor"),
            P("context", "tensor"),
            P("context", "tensor"),
            P("context", "tensor"),
            P("tensor"),
            P("tensor", None),
        ),
        out_specs=P("context", "tensor"),
        check_vma=False,
    )
```

```python
import jax
import jax.numpy as jnp
from jax import lax
from jax.experimental import pallas as pl
from jax.experimental.pallas import tpu as pltpu
from jax.sharding import Mesh, PartitionSpec as P

BLOCK = 128
SLOTS = 10
TENSOR = ("x_far", "x_near", "y_near")
PAIR = "x_near"
PIECES = 8
SHARE = 16
F32 = jnp.float32
BF16 = jnp.bfloat16


def iota(shape, axis):
    return lax.broadcasted_iota(jnp.int32, shape, axis)


def nt_dot(a, b):
    return lax.dot_general(a, b, (((1,), (1,)), ((), ())), preferred_element_type=F32)


def fold(ref, start, block):
    for k in range(BLOCK // SHARE):
        ref[start : start + SHARE, k * block.shape[1] : (k + 1) * block.shape[1]] = block[k * SHARE : (k + 1) * SHARE]


def unfold(ref, start, width):
    return jnp.concatenate([ref[start : start + SHARE, k * width : (k + 1) * width] for k in range(BLOCK // SHARE)], axis=0)


def pack_kernel(*refs):
    sources, projection, (out_ref, direct_ref, own_gate_ref, leaving_ref), refs = refs[:5], refs[5], refs[6:10], refs[10:]
    in_gate_ref, values_ref, filters_ref, skip_ref, out_gate_ref, rows_ref, sems = refs
    targets = (in_gate_ref, values_ref, filters_ref, skip_ref, out_gate_ref)
    moves = [pltpu.make_async_copy(sources[n], targets[n], sems.at[n]) for n in range(5)]
    for move in moves:
        move.start()
    depth = projection.shape[0]
    share = depth // PIECES
    copied = [
        pltpu.make_async_copy(
            projection.at[n * share : (n + 1) * share], leaving_ref.at[n * share : (n + 1) * share], sems.at[5 + n]
        )
        for n in range(PIECES)
    ]
    for move in copied:
        move.start()
    rows, width = in_gate_ref.shape
    groups = filters_ref.shape[0]
    peers = out_ref.shape[0] // SLOTS
    chans = width // peers
    row, col = iota((peers * 8, width), 0), iota((peers * 8, width), 1)
    picks = [
        ((row % 8 // chans == b) & (row // 8 * chans + row % chans == col)).astype(F32).astype(BF16) for b in range(2)
    ]
    for move in moves:
        move.wait()
    products = in_gate_ref[...].astype(F32) * values_ref[...].astype(F32)
    direct = skip_ref[...] * products
    first = lax.axis_index(PAIR) == 0
    low, high = direct[:BLOCK], direct[BLOCK:]
    direct_ref[...] = jnp.where(first, low, high)
    fold(leaving_ref, depth, jnp.where(first, high, low).astype(BF16))
    low, high = out_gate_ref[:BLOCK].astype(F32), out_gate_ref[BLOCK:].astype(F32)
    own_gate_ref[...] = jnp.where(first, low, high).astype(BF16)
    fold(leaving_ref, depth + SHARE, jnp.where(first, high, low).astype(BF16))
    mixed = products.astype(BF16)
    sent = sum(nt_dot(picks[b], mixed[b * BLOCK : (b + 1) * BLOCK]) for b in range(2))
    for j in range(peers):
        rows_ref[j * SLOTS : j * SLOTS + 8, :] = sent[j * 8 : j * 8 + 8]
        g = j // (peers // groups)
        for b in range(2):
            rows_ref[j * SLOTS + 8 + b : j * SLOTS + 9 + b, :] = filters_ref[g : g + 1, b * BLOCK : (b + 1) * BLOCK]
    out_ref[...] = rows_ref[...].astype(BF16)
    for move in copied:
        move.wait()


def conv_kernel(in_ref, out_ref, lhs_ref, acc_ref, tap_ref):
    peers = in_ref.shape[0] // SLOTS
    blocks = 2 * peers
    rows = 4 * blocks
    tap_ref[...] = in_ref[...].astype(F32)
    x = jnp.concatenate([tap_ref[k * SLOTS : k * SLOTS + 8, :] for k in range(peers)], axis=0)
    for m in range(4):
        moved = x if m == 0 else jnp.concatenate([jnp.zeros((4 * m, BLOCK), F32), x[: rows - 4 * m]], axis=0)
        lhs_ref[:, m * BLOCK : (m + 1) * BLOCK] = moved.astype(BF16)
    acc_ref[...] = jnp.zeros_like(acc_ref)
    keep = iota((BLOCK, BLOCK), 1) >= iota((BLOCK, BLOCK), 0)

    def turned(block):
        if block < 0:
            return jnp.zeros((BLOCK, BLOCK), F32)
        place = (block // 2) * SLOTS + 8 + block % 2
        taps = jnp.broadcast_to(tap_ref[place : place + 1, :], (BLOCK, BLOCK))
        return pltpu.roll(taps, 0, 1, stride=1, stride_axis=0)

    step = blocks // 8
    for first in range(0, blocks, 2 * step):
        last = [turned(first - 1), turned(first + step - 1)]
        for q in range(first, first + step, 4):
            sides = []
            for side in range(2):
                stack = []
                for m in range(4):
                    now = turned(q + side * step + m)
                    stack.append(jnp.where(keep, now, last[side]).astype(BF16))
                    last[side] = now
                sides.append(jnp.concatenate(stack, axis=0))
            both = jnp.concatenate(sides, axis=1)
            acc_ref[4 * q :, :] += jnp.dot(lhs_ref[: rows - 4 * q, :], both, preferred_element_type=F32)
    moved = 4 * step
    out_ref[:moved, :] = acc_ref[:moved, :BLOCK].astype(BF16)
    out_ref[moved:, :] = (acc_ref[moved:, :BLOCK] + acc_ref[: rows - moved, BLOCK:]).astype(BF16)


def project_kernel(conv_ref, direct_ref, own_gate_ref, own_rows_ref, given_ref, out_ref):
    width = direct_ref.shape[1]
    depth = own_rows_ref.shape[0] - 2 * SHARE
    received = conv_ref[...].astype(F32).T.astype(BF16)
    here = lax.axis_index(PAIR)
    gated = []
    for side, direct, gate in (
        (here, direct_ref[...], own_gate_ref[...]),
        (1 - here, unfold(given_ref, depth, width).astype(F32), unfold(given_ref, depth + SHARE, width)),
    ):
        row, col = iota((2 * width, width), 0), iota((2 * width, width), 1)
        pick = (row % 8 // 4 == side) & (row // 8 * 4 + row % 4 == col)
        conv = jnp.dot(received, pick.astype(F32).astype(BF16), preferred_element_type=F32)
        gated.append(((conv + direct) * gate.astype(F32)).astype(BF16))
    for k in range(out_ref.shape[0]):
        total = jnp.dot(gated[0], own_rows_ref[:depth, k * width : (k + 1) * width], preferred_element_type=F32)
        total += jnp.dot(gated[1], given_ref[:depth, k * width : (k + 1) * width], preferred_element_type=F32)
        out_ref[k] = total.astype(BF16)


def sum_kernel(parts_ref, out_ref):
    step = {"x_far": 4, "x_near": 2, "y_near": 1}[PAIR]
    for side in range(2):
        total = None
        for k in range(parts_ref.shape[0]):
            if k // step % 2 == side:
                part = parts_ref[k].astype(F32)
                total = part if total is None else total + part
        out_ref[side * BLOCK : (side + 1) * BLOCK, :] = total.astype(BF16)


def call(kernel, shape, *args, scratch=(), cost=None):
    return pl.pallas_call(
        kernel,
        out_shape=jax.ShapeDtypeStruct(shape, BF16),
        scratch_shapes=scratch,
        cost_estimate=cost,
        compiler_params=pltpu.CompilerParams(vmem_limit_bytes=32 * 1024 * 1024),
    )(*args)


def on_device(in_gate, out_gate, values, long_filters, skip_gain, projection):
    rows, width = in_gate.shape
    contexts = lax.axis_size("context")
    tensors = lax.axis_size(TENSOR)
    args = (in_gate, values, long_filters.T, skip_gain[None, :], out_gate, projection)
    sent, direct, own_gate, leaving = pl.pallas_call(
        pack_kernel,
        in_specs=[pl.BlockSpec(memory_space=pltpu.HBM)] * len(args),
        out_shape=[
            jax.ShapeDtypeStruct((contexts * SLOTS, BLOCK), BF16),
            jax.ShapeDtypeStruct((BLOCK, width), F32),
            jax.ShapeDtypeStruct((BLOCK, width), BF16),
            jax.ShapeDtypeStruct((projection.shape[0] + 2 * SHARE, projection.shape[1]), BF16),
        ],
        scratch_shapes=[
            pltpu.VMEM((rows, width), BF16),
            pltpu.VMEM((rows, width), BF16),
            pltpu.VMEM((long_filters.shape[1], rows), F32),
            pltpu.VMEM((1, width), F32),
            pltpu.VMEM((rows, width), BF16),
            pltpu.VMEM((contexts * SLOTS, BLOCK), F32),
            pltpu.SemaphoreType.DMA((len(args) - 1 + PIECES,)),
        ],
        compiler_params=pltpu.CompilerParams(vmem_limit_bytes=32 * 1024 * 1024),
    )(*(pltpu.with_memory_space_constraint(a, pltpu.HBM) for a in args))
    held = lax.all_to_all(sent.reshape(contexts * SLOTS // 2, 2, BLOCK), "context", 0, 0, tiled=True)
    conv = call(
        conv_kernel,
        (contexts * 8, BLOCK),
        held.reshape(contexts * SLOTS, BLOCK),
        cost=pl.CostEstimate(flops=8000000000, bytes_accessed=300000, transcendentals=0),
        scratch=[
            pltpu.VMEM((contexts * 8, 4 * BLOCK), BF16),
            pltpu.VMEM((contexts * 8, 2 * BLOCK), F32),
            pltpu.VMEM((contexts * SLOTS, BLOCK), F32),
        ],
    )
    given = lax.ppermute(leaving, PAIR, [(0, 1), (1, 0)])
    back = lax.all_to_all(conv.reshape(2 * contexts, 4, BLOCK), ("context", PAIR), 0, 0, tiled=True)
    partial = call(
        project_kernel,
        (tensors, BLOCK, width),
        back.reshape(contexts * 8, BLOCK),
        direct,
        own_gate,
        leaving,
        given,
    )
    shares = lax.all_to_all(partial, TENSOR, 0, 0, tiled=True)
    return call(sum_kernel, (rows, width), shares)


def solution(mesh):
    contexts = mesh.shape["context"]
    fine = Mesh(mesh.devices.reshape(contexts, 2, 2, 2), ("context",) + TENSOR)
    return jax.shard_map(
        on_device,
        mesh=fine,
        in_specs=(
            P("context", TENSOR),
            P("context", TENSOR),
            P("context", TENSOR),
            P("context", TENSOR),
            P(TENSOR),
            P(TENSOR, None),
        ),
        out_specs=P("context", TENSOR),
        check_vma=False,
    )
```

```python
import jax
import jax.numpy as jnp
from jax import lax
from jax.experimental import pallas as pl
from jax.experimental.pallas import tpu as pltpu
from jax.sharding import Mesh, PartitionSpec as P

BLOCK = 128
SLOTS = 10
Y_FAR = 4
CONTEXT = ("y_far", "line")
TENSOR = ("x_far", "x_near", "y_near")
PAIR = "y_near"
PIECES = 8
SHARE = 16
F32 = jnp.float32
BF16 = jnp.bfloat16


def iota(shape, axis):
    return lax.broadcasted_iota(jnp.int32, shape, axis)


def nt_dot(a, b):
    return lax.dot_general(a, b, (((1,), (1,)), ((), ())), preferred_element_type=F32)


def fold(ref, start, block):
    for k in range(BLOCK // SHARE):
        ref[start : start + SHARE, k * block.shape[1] : (k + 1) * block.shape[1]] = block[k * SHARE : (k + 1) * SHARE]


def unfold(ref, start, width):
    return jnp.concatenate([ref[start : start + SHARE, k * width : (k + 1) * width] for k in range(BLOCK // SHARE)], axis=0)


def pack_kernel(*refs):
    sources, projection, outs, refs = refs[:5], refs[5], refs[6:11], refs[11:]
    out_ref, direct_ref, own_gate_ref, leaving_ref, leaving_back_ref = outs
    in_gate_ref, values_ref, filters_ref, skip_ref, out_gate_ref, rows_ref, sems = refs
    targets = (in_gate_ref, values_ref, filters_ref, skip_ref, out_gate_ref)
    moves = [pltpu.make_async_copy(sources[n], targets[n], sems.at[n]) for n in range(5)]
    for move in moves:
        move.start()
    depth = projection.shape[0] // 2
    share = 2 * depth // PIECES
    copied = []
    for n in range(PIECES):
        start = n * share
        holder, at = (leaving_ref, start) if start < depth else (leaving_back_ref, start - depth)
        target = holder.at[at : at + share]
        copied.append(pltpu.make_async_copy(projection.at[start : start + share], target, sems.at[5 + n]))
    for move in copied:
        move.start()
    rows, width = in_gate_ref.shape
    groups = filters_ref.shape[0]
    peers = out_ref.shape[0] // SLOTS
    chans = width // peers
    row, col = iota((peers * 8, width), 0), iota((peers * 8, width), 1)
    picks = [
        ((row % 8 // chans == b) & (row // 8 * chans + row % chans == col)).astype(F32).astype(BF16) for b in range(2)
    ]
    for move in moves:
        move.wait()
    products = in_gate_ref[...].astype(F32) * values_ref[...].astype(F32)
    direct = skip_ref[...] * products
    first = lax.axis_index(PAIR) == 0
    low, high = direct[:BLOCK], direct[BLOCK:]
    direct_ref[...] = jnp.where(first, low, high)
    fold(leaving_ref, depth, jnp.where(first, high, low).astype(BF16))
    low, high = out_gate_ref[:BLOCK].astype(F32), out_gate_ref[BLOCK:].astype(F32)
    own_gate_ref[...] = jnp.where(first, low, high).astype(BF16)
    fold(leaving_ref, depth + SHARE, jnp.where(first, high, low).astype(BF16))
    mixed = products.astype(BF16)
    sent = sum(nt_dot(picks[b], mixed[b * BLOCK : (b + 1) * BLOCK]) for b in range(2))
    for j in range(peers):
        rows_ref[j * SLOTS : j * SLOTS + 8, :] = sent[j * 8 : j * 8 + 8]
        g = j // (peers // groups)
        for b in range(2):
            rows_ref[j * SLOTS + 8 + b : j * SLOTS + 9 + b, :] = filters_ref[g : g + 1, b * BLOCK : (b + 1) * BLOCK]
    out_ref[...] = rows_ref[...].astype(BF16)
    for move in copied:
        move.wait()


def conv_kernel(in_ref, out_ref, lhs_ref, acc_ref, tap_ref):
    peers = in_ref.shape[0] // SLOTS
    blocks = 2 * peers
    rows = 4 * blocks
    tap_ref[...] = in_ref[...].astype(F32)
    x = jnp.concatenate([tap_ref[k * SLOTS : k * SLOTS + 8, :] for k in range(peers)], axis=0)
    for m in range(4):
        moved = x if m == 0 else jnp.concatenate([jnp.zeros((4 * m, BLOCK), F32), x[: rows - 4 * m]], axis=0)
        lhs_ref[:, m * BLOCK : (m + 1) * BLOCK] = moved.astype(BF16)
    acc_ref[...] = jnp.zeros_like(acc_ref)
    keep = iota((BLOCK, BLOCK), 1) >= iota((BLOCK, BLOCK), 0)

    def turned(block):
        if block < 0:
            return jnp.zeros((BLOCK, BLOCK), F32)
        place = (block // 2) * SLOTS + 8 + block % 2
        taps = jnp.broadcast_to(tap_ref[place : place + 1, :], (BLOCK, BLOCK))
        return pltpu.roll(taps, 0, 1, stride=1, stride_axis=0)

    step = blocks // 8
    for first in range(0, blocks, 2 * step):
        last = [turned(first - 1), turned(first + step - 1)]
        for q in range(first, first + step, 4):
            sides = []
            for side in range(2):
                stack = []
                for m in range(4):
                    now = turned(q + side * step + m)
                    stack.append(jnp.where(keep, now, last[side]).astype(BF16))
                    last[side] = now
                sides.append(jnp.concatenate(stack, axis=0))
            both = jnp.concatenate(sides, axis=1)
            acc_ref[4 * q :, :] += jnp.dot(lhs_ref[: rows - 4 * q, :], both, preferred_element_type=F32)
    moved = 4 * step
    out_ref[:moved, :] = acc_ref[:moved, :BLOCK].astype(BF16)
    out_ref[moved:, :] = (acc_ref[moved:, :BLOCK] + acc_ref[: rows - moved, BLOCK:]).astype(BF16)


def gate_kernel(conv_ref, direct_ref, own_gate_ref, given_ref, out_ref):
    width = direct_ref.shape[1]
    depth = given_ref.shape[0] - 2 * SHARE
    received = conv_ref[...].astype(F32).T.astype(BF16)
    here = lax.axis_index(PAIR)
    for n, (side, direct, gate) in enumerate(
        (
            (here, direct_ref[...], own_gate_ref[...]),
            (1 - here, unfold(given_ref, depth, width).astype(F32), unfold(given_ref, depth + SHARE, width)),
        )
    ):
        row, col = iota((2 * width, width), 0), iota((2 * width, width), 1)
        pick = (row % 8 // 4 == side) & (row // 8 * 4 + row % 4 == col)
        conv = jnp.dot(received, pick.astype(F32).astype(BF16), preferred_element_type=F32)
        out_ref[:, n * width : (n + 1) * width] = ((conv + direct) * gate.astype(F32)).astype(BF16)


def project_kernel(gated_ref, own_ref, own_back_ref, given_ref, given_back_ref, out_ref):
    width = out_ref.shape[2]
    depth = own_back_ref.shape[0]
    own_gated, given_gated = gated_ref[:, :width], gated_ref[:, width:]
    for k in range(out_ref.shape[0]):
        part = slice(k * width, (k + 1) * width)
        own = jnp.concatenate([own_ref[:depth, part], own_back_ref[:, part]], axis=0)
        given = jnp.concatenate([given_ref[:depth, part], given_back_ref[:, part]], axis=0)
        total = jnp.dot(own_gated, own, preferred_element_type=F32)
        total += jnp.dot(given_gated, given, preferred_element_type=F32)
        out_ref[k] = total.astype(BF16)


def sum_kernel(parts_ref, out_ref):
    step = {"x_far": 4, "x_near": 2, "y_near": 1}[PAIR]
    for side in range(2):
        total = None
        for k in range(parts_ref.shape[0]):
            if k // step % 2 == side:
                part = parts_ref[k].astype(F32)
                total = part if total is None else total + part
        out_ref[side * BLOCK : (side + 1) * BLOCK, :] = total.astype(BF16)


def call(kernel, shape, *args, scratch=(), cost=None):
    return pl.pallas_call(
        kernel,
        out_shape=jax.ShapeDtypeStruct(shape, BF16),
        scratch_shapes=scratch,
        cost_estimate=cost,
        compiler_params=pltpu.CompilerParams(vmem_limit_bytes=32 * 1024 * 1024),
    )(*args)


def on_device(in_gate, out_gate, values, long_filters, skip_gain, projection):
    rows, width = in_gate.shape
    contexts = lax.axis_size(CONTEXT)
    tensors = lax.axis_size(TENSOR)
    args = (in_gate, values, long_filters.T, skip_gain[None, :], out_gate, projection)
    sent, direct, own_gate, leaving, leaving_back = pl.pallas_call(
        pack_kernel,
        in_specs=[pl.BlockSpec(memory_space=pltpu.HBM)] * len(args),
        out_shape=[
            jax.ShapeDtypeStruct((contexts * SLOTS, BLOCK), BF16),
            jax.ShapeDtypeStruct((BLOCK, width), F32),
            jax.ShapeDtypeStruct((BLOCK, width), BF16),
            jax.ShapeDtypeStruct((projection.shape[0] // 2 + 2 * SHARE, projection.shape[1]), BF16),
            jax.ShapeDtypeStruct((projection.shape[0] // 2, projection.shape[1]), BF16),
        ],
        scratch_shapes=[
            pltpu.VMEM((rows, width), BF16),
            pltpu.VMEM((rows, width), BF16),
            pltpu.VMEM((long_filters.shape[1], rows), F32),
            pltpu.VMEM((1, width), F32),
            pltpu.VMEM((rows, width), BF16),
            pltpu.VMEM((contexts * SLOTS, BLOCK), F32),
            pltpu.SemaphoreType.DMA((len(args) - 1 + PIECES,)),
        ],
        compiler_params=pltpu.CompilerParams(vmem_limit_bytes=32 * 1024 * 1024),
    )(*(pltpu.with_memory_space_constraint(a, pltpu.HBM) for a in args))
    held = lax.all_to_all(sent.reshape(contexts * SLOTS // 2, 2, BLOCK), CONTEXT, 0, 0, tiled=True)
    conv = call(
        conv_kernel,
        (contexts * 8, BLOCK),
        held.reshape(contexts * SLOTS, BLOCK),
        cost=pl.CostEstimate(flops=8000000000, bytes_accessed=300000, transcendentals=0),
        scratch=[
            pltpu.VMEM((contexts * 8, 4 * BLOCK), BF16),
            pltpu.VMEM((contexts * 8, 2 * BLOCK), F32),
            pltpu.VMEM((contexts * SLOTS, BLOCK), F32),
        ],
    )
    given = lax.ppermute(leaving, PAIR, [(0, 1), (1, 0)])
    places = 2 * Y_FAR
    around = [(i, (i + 1) % places if i % 2 else (i - 1) % places) for i in range(places)]
    given_back = lax.ppermute(leaving_back, ("y_far", PAIR), around)
    back = lax.all_to_all(conv.reshape(2 * contexts, 4, BLOCK), CONTEXT + (PAIR,), 0, 0, tiled=True)
    gated = call(gate_kernel, (BLOCK, 2 * width), back.reshape(contexts * 8, BLOCK), direct, own_gate, given)
    partial = call(
        project_kernel,
        (tensors, BLOCK, width),
        gated,
        leaving,
        leaving_back,
        given,
        given_back,
    )
    shares = lax.all_to_all(partial, TENSOR, 0, 0, tiled=True)
    return call(sum_kernel, (rows, width), shares)


def solution(mesh):
    lines = mesh.shape["context"] // Y_FAR
    fine = Mesh(mesh.devices.reshape(Y_FAR, lines, 2, 2, 2), CONTEXT + TENSOR)
    return jax.shard_map(
        on_device,
        mesh=fine,
        in_specs=(
            P(CONTEXT, TENSOR),
            P(CONTEXT, TENSOR),
            P(CONTEXT, TENSOR),
            P(CONTEXT, TENSOR),
            P(TENSOR),
            P(TENSOR, None),
        ),
        out_specs=P(CONTEXT, TENSOR),
        check_vma=False,
    )
```

```python
import jax
import jax.numpy as jnp
from jax import lax
from jax.experimental import pallas as pl
from jax.experimental.pallas import tpu as pltpu
from jax.sharding import Mesh, PartitionSpec as P

BLOCK = 128
SLOTS = 10
Y_FAR = 4
CONTEXT = ("y_far", "line")
TENSOR = ("x_far", "x_near", "y_near")
PAIR = "y_near"
PIECES = 2
SHARE = 16
F32 = jnp.float32
BF16 = jnp.bfloat16


def iota(shape, axis):
    return lax.broadcasted_iota(jnp.int32, shape, axis)


def nt_dot(a, b):
    return lax.dot_general(a, b, (((1,), (1,)), ((), ())), preferred_element_type=F32)


def fold(ref, start, block):
    for k in range(BLOCK // SHARE):
        ref[start : start + SHARE, k * block.shape[1] : (k + 1) * block.shape[1]] = block[k * SHARE : (k + 1) * SHARE]


def unfold(ref, start, width):
    return jnp.concatenate([ref[start : start + SHARE, k * width : (k + 1) * width] for k in range(BLOCK // SHARE)], axis=0)


def pack_kernel(*refs):
    sources, projection, outs, refs = refs[:5], refs[5], refs[6:11], refs[11:]
    out_ref, direct_ref, own_gate_ref, leaving_ref, leaving_back_ref = outs
    in_gate_ref, values_ref, filters_ref, skip_ref, out_gate_ref, rows_ref, sems = refs
    targets = (in_gate_ref, values_ref, filters_ref, skip_ref, out_gate_ref)
    moves = [pltpu.make_async_copy(sources[n], targets[n], sems.at[n]) for n in range(5)]
    for move in moves:
        move.start()
    depth = projection.shape[0] // 2
    share = 2 * depth // PIECES
    copied = []
    for n in range(PIECES):
        start = n * share
        holder, at = (leaving_ref, start) if start < depth else (leaving_back_ref, start - depth)
        target = holder.at[at : at + share]
        copied.append(pltpu.make_async_copy(projection.at[start : start + share], target, sems.at[5 + n]))
    for move in copied:
        move.start()
    rows, width = in_gate_ref.shape
    groups = filters_ref.shape[0]
    peers = out_ref.shape[0] // SLOTS
    chans = width // peers
    row, col = iota((peers * 8, width), 0), iota((peers * 8, width), 1)
    picks = [
        ((row % 8 // chans == b) & (row // 8 * chans + row % chans == col)).astype(F32).astype(BF16) for b in range(2)
    ]
    for move in moves:
        move.wait()
    products = in_gate_ref[...].astype(F32) * values_ref[...].astype(F32)
    direct = skip_ref[...] * products
    first = lax.axis_index(PAIR) == 0
    low, high = direct[:BLOCK], direct[BLOCK:]
    direct_ref[...] = jnp.where(first, low, high)
    fold(leaving_ref, depth, jnp.where(first, high, low).astype(BF16))
    low, high = out_gate_ref[:BLOCK].astype(F32), out_gate_ref[BLOCK:].astype(F32)
    own_gate_ref[...] = jnp.where(first, low, high).astype(BF16)
    fold(leaving_ref, depth + SHARE, jnp.where(first, high, low).astype(BF16))
    mixed = products.astype(BF16)
    sent = sum(nt_dot(picks[b], mixed[b * BLOCK : (b + 1) * BLOCK]) for b in range(2))
    for j in range(peers):
        rows_ref[j * SLOTS : j * SLOTS + 8, :] = sent[j * 8 : j * 8 + 8]
        g = j // (peers // groups)
        for b in range(2):
            rows_ref[j * SLOTS + 8 + b : j * SLOTS + 9 + b, :] = filters_ref[g : g + 1, b * BLOCK : (b + 1) * BLOCK]
    out_ref[...] = rows_ref[...].astype(BF16)
    for move in copied:
        move.wait()


def conv_kernel(in_ref, out_ref, lhs_ref, acc_ref, tap_ref):
    peers = in_ref.shape[0] // SLOTS
    blocks = 2 * peers
    rows = 4 * blocks
    tap_ref[...] = in_ref[...].astype(F32)
    x = jnp.concatenate([tap_ref[k * SLOTS : k * SLOTS + 8, :] for k in range(peers)], axis=0)
    for m in range(4):
        moved = x if m == 0 else jnp.concatenate([jnp.zeros((4 * m, BLOCK), F32), x[: rows - 4 * m]], axis=0)
        lhs_ref[:, m * BLOCK : (m + 1) * BLOCK] = moved.astype(BF16)
    keep = iota((BLOCK, BLOCK), 1) >= iota((BLOCK, BLOCK), 0)

    def turned(block):
        if block < 0:
            return jnp.zeros((BLOCK, BLOCK), F32)
        place = (block // 2) * SLOTS + 8 + block % 2
        taps = jnp.broadcast_to(tap_ref[place : place + 1, :], (BLOCK, BLOCK))
        return pltpu.roll(taps, 0, 1, stride=1, stride_axis=0)

    step = blocks // 8
    for first in range(0, blocks, 2 * step):
        last = [turned(first - 1), turned(first + step - 1)]
        for q in range(first, first + step, 4):
            sides = []
            for side in range(2):
                stack = []
                for m in range(4):
                    now = turned(q + side * step + m)
                    stack.append(jnp.where(keep, now, last[side]).astype(BF16))
                    last[side] = now
                sides.append(jnp.concatenate(stack, axis=0))
            both = jnp.concatenate(sides, axis=1)
            part = jnp.dot(lhs_ref[: rows - 4 * q, :], both, preferred_element_type=F32)
            if q == 0:
                acc_ref[...] = part
            else:
                acc_ref[4 * q :, :] += part
    moved = 4 * step
    out_ref[:moved, :] = acc_ref[:moved, :BLOCK].astype(BF16)
    out_ref[moved:, :] = (acc_ref[moved:, :BLOCK] + acc_ref[: rows - moved, BLOCK:]).astype(BF16)


def gate_kernel(conv_ref, direct_ref, own_gate_ref, given_ref, out_ref):
    width = direct_ref.shape[1]
    depth = given_ref.shape[0] - 2 * SHARE
    received = conv_ref[...].astype(F32).T.astype(BF16)
    here = lax.axis_index(PAIR)
    for n, (side, direct, gate) in enumerate(
        (
            (here, direct_ref[...], own_gate_ref[...]),
            (1 - here, unfold(given_ref, depth, width).astype(F32), unfold(given_ref, depth + SHARE, width)),
        )
    ):
        row, col = iota((2 * width, width), 0), iota((2 * width, width), 1)
        pick = (row % 8 // 4 == side) & (row // 8 * 4 + row % 4 == col)
        conv = jnp.dot(received, pick.astype(F32).astype(BF16), preferred_element_type=F32)
        out_ref[:, n * width : (n + 1) * width] = ((conv + direct) * gate.astype(F32)).astype(BF16)


def project_kernel(gated_ref, own_ref, own_back_ref, given_ref, given_back_ref, out_ref):
    width = out_ref.shape[2]
    depth = own_back_ref.shape[0]
    own_gated, given_gated = gated_ref[:, :width], gated_ref[:, width:]
    for k in range(out_ref.shape[0]):
        part = slice(k * width, (k + 1) * width)
        own = jnp.concatenate([own_ref[:depth, part], own_back_ref[:, part]], axis=0)
        given = jnp.concatenate([given_ref[:depth, part], given_back_ref[:, part]], axis=0)
        total = jnp.dot(own_gated, own, preferred_element_type=F32)
        total += jnp.dot(given_gated, given, preferred_element_type=F32)
        out_ref[k] = total.astype(BF16)


def sum_kernel(parts_ref, out_hbm, total_ref, sems):
    step = {"x_far": 4, "x_near": 2, "y_near": 1}[PAIR]
    moves = []
    for side in range(2):
        total = None
        for k in range(parts_ref.shape[0]):
            if k // step % 2 == side:
                part = parts_ref[k].astype(F32)
                total = part if total is None else total + part
        half = pl.ds(side * BLOCK, BLOCK)
        total_ref[half, :] = total.astype(BF16)
        moves.append(pltpu.make_async_copy(total_ref.at[half], out_hbm.at[half], sems.at[side]))
        moves[-1].start()
    for move in moves:
        move.wait()


def call(kernel, shape, *args, scratch=(), cost=None):
    return pl.pallas_call(
        kernel,
        out_shape=jax.ShapeDtypeStruct(shape, BF16),
        scratch_shapes=scratch,
        cost_estimate=cost,
        compiler_params=pltpu.CompilerParams(vmem_limit_bytes=32 * 1024 * 1024),
    )(*args)


def on_device(in_gate, out_gate, values, long_filters, skip_gain, projection):
    rows, width = in_gate.shape
    contexts = lax.axis_size(CONTEXT)
    tensors = lax.axis_size(TENSOR)
    args = (in_gate, values, long_filters.T, skip_gain[None, :], out_gate, projection)
    sent, direct, own_gate, leaving, leaving_back = pl.pallas_call(
        pack_kernel,
        in_specs=[pl.BlockSpec(memory_space=pltpu.HBM)] * len(args),
        out_shape=[
            jax.ShapeDtypeStruct((contexts * SLOTS, BLOCK), BF16),
            jax.ShapeDtypeStruct((BLOCK, width), F32),
            jax.ShapeDtypeStruct((BLOCK, width), BF16),
            jax.ShapeDtypeStruct((projection.shape[0] // 2 + 2 * SHARE, projection.shape[1]), BF16),
            jax.ShapeDtypeStruct((projection.shape[0] // 2, projection.shape[1]), BF16),
        ],
        scratch_shapes=[
            pltpu.VMEM((rows, width), BF16),
            pltpu.VMEM((rows, width), BF16),
            pltpu.VMEM((long_filters.shape[1], rows), F32),
            pltpu.VMEM((1, width), F32),
            pltpu.VMEM((rows, width), BF16),
            pltpu.VMEM((contexts * SLOTS, BLOCK), F32),
            pltpu.SemaphoreType.DMA((len(args) - 1 + PIECES,)),
        ],
        compiler_params=pltpu.CompilerParams(vmem_limit_bytes=32 * 1024 * 1024),
    )(*(pltpu.with_memory_space_constraint(a, pltpu.HBM) for a in args))
    held = lax.all_to_all(sent.reshape(contexts * SLOTS // 2, 2, BLOCK), CONTEXT, 0, 0, tiled=True)
    conv = call(
        conv_kernel,
        (contexts * 8, BLOCK),
        held.reshape(contexts * SLOTS, BLOCK),
        cost=pl.CostEstimate(flops=8000000000, bytes_accessed=300000, transcendentals=0),
        scratch=[
            pltpu.VMEM((contexts * 8, 4 * BLOCK), BF16),
            pltpu.VMEM((contexts * 8, 2 * BLOCK), F32),
            pltpu.VMEM((contexts * SLOTS, BLOCK), F32),
        ],
    )
    given = lax.ppermute(leaving, PAIR, [(0, 1), (1, 0)])
    places = 2 * Y_FAR
    around = [(i, (i + 1) % places if i % 2 else (i - 1) % places) for i in range(places)]
    given_back = lax.ppermute(leaving_back, ("y_far", PAIR), around)
    back = lax.all_to_all(conv.reshape(2 * contexts, 4, BLOCK), CONTEXT + (PAIR,), 0, 0, tiled=True)
    gated = call(gate_kernel, (BLOCK, 2 * width), back.reshape(contexts * 8, BLOCK), direct, own_gate, given)
    partial = call(
        project_kernel,
        (tensors, BLOCK, width),
        gated,
        leaving,
        leaving_back,
        given,
        given_back,
    )
    shares = lax.all_to_all(partial, TENSOR, 0, 0, tiled=True)
    return pl.pallas_call(
        sum_kernel,
        out_shape=pltpu.HBM((rows, width), BF16),
        out_specs=pl.BlockSpec(memory_space=pltpu.HBM),
        scratch_shapes=[pltpu.VMEM((rows, width), BF16), pltpu.SemaphoreType.DMA((2,))],
        compiler_params=pltpu.CompilerParams(vmem_limit_bytes=32 * 1024 * 1024),
    )(shares)


def solution(mesh):
    lines = mesh.shape["context"] // Y_FAR
    fine = Mesh(mesh.devices.reshape(Y_FAR, lines, 2, 2, 2), CONTEXT + TENSOR)
    return jax.shard_map(
        on_device,
        mesh=fine,
        in_specs=(
            P(CONTEXT, TENSOR),
            P(CONTEXT, TENSOR),
            P(CONTEXT, TENSOR),
            P(CONTEXT, TENSOR),
            P(TENSOR),
            P(TENSOR, None),
        ),
        out_specs=P(CONTEXT, TENSOR),
        check_vma=False,
    )
```
